128 devices in a mesh: dp: 8 (over x, core), tensor: 4 (over z), group: 4 (over y).
Axes of the slice: x: 4, y: 4, z: 4, core: 2. Of those that a mesh axis runs over, the one named last changes fastest.
Arguments:
- attn_heads: bfloat16 [2048, 8192], P(('dp', 'group'), 'tensor'), may hold values from -6 to 6
- out_proj: bfloat16 [8192, 8192], P('tensor', ('dp', 'group')), may hold values from -0.0625 to 0.0625
- low_tap: bfloat16 [2048, 8192], P('tensor', ('dp', 'group')), may hold values from -6 to 6
- mid_tap: bfloat16 [2048, 8192], P('tensor', ('dp', 'group')), may hold values from -6 to 6
- join_weight: bfloat16 [3, 8192, 8192], P(None, ('dp', 'group'), 'tensor'), may hold values from -0.0390625 to 0.0390625
- norm_gain: float32 [8192], P('tensor'), may hold values from 0.5 to 1.5
- head_weight: bfloat16 [8192, 32000], P('tensor', ('dp', 'group')), may hold values from -8 to 8
- targets: int32 [2048], P('tensor'), may hold values from 0 to 31999
- loss_mask: int32 [2048], P('tensor'), may hold values 0 or 1
Outputs:
- draft_hidden: bfloat16 [2048, 8192], P(('dp', 'group'), 'tensor')
- row_loss: float32 [2048], P('tensor')
The draws below stay inside these ranges and needn't reach their ends.
All inputs are finite; a program needn't handle non-finite values. No bound on the sum of `loss_mask` on one device may be relied on, other than what follows from the above.
Results may differ from the reference program's by a relative error of at most 0.012.
Values may be sent and summed in bfloat16 or wider, within the bound.
A program may use at most 128 MiB of HBM per device.

```python
import math
import jax
import jax.numpy as jnp
import numpy as np
from jax import lax

D = 8192
VOCAB = 32000
TOKENS = 2048


def draw_head_weight(key, part):
    key = jax.random.fold_in(key, 11)
    first = jax.random.fold_in(key, 0)
    base_scale = 3.0 / jnp.sqrt(jnp.float32(D))
    values = jax.random.normal(first, (D, VOCAB), jnp.float32)
    return jnp.clip(values * base_scale, -8.0, 8.0).astype(jnp.bfloat16)


def set_ends(entries, stream_key, least, top_value):
    index_at = [jax.random.randint(jax.random.fold_in(stream_key, axis), (), 0, length) for axis, length in enumerate(entries.shape)]
    main_axis = entries.shape.index(max(entries.shape))
    next_to = index_at[:main_axis] + [(index_at[main_axis] + 1) % entries.shape[main_axis]] + index_at[main_axis + 1:]
    return entries.at[tuple(index_at)].set(least).at[tuple(next_to)].set(top_value)


def level_of(key, shape, shards, low, top_value):
    loudness = 1.0
    for dim, parts in shards:
        heights = jax.random.uniform(jax.random.fold_in(jax.random.fold_in(key, 6), dim), (parts,), jnp.float32, low / len(shards), top_value / len(shards))
        loudness = loudness * jnp.repeat(jnp.exp(heights), shape[dim] // parts).reshape((-1,) + (1,) * (len(shape) - 1 - dim))
    return loudness


def cumulative_ranks(number_of, skew):
    loads = [(1 << 20) // math.isqrt(grade ** skew) + 1 for grade in range(1, number_of + 1)]
    width = 1 + sum(loads) // (1 << 30)
    return np.cumsum(np.array([max(1, weight // width) for weight in loads]))


def skewed_ids(rng, extent, number_of, slope):
    listing = cumulative_ranks(number_of, slope)
    lot = jax.random.randint(jax.random.fold_in(rng, 1), extent, 0, int(listing[number_of - 1]))
    rank = jnp.searchsorted(jnp.asarray(listing, jnp.int32), lot, side="right")
    return jax.random.permutation(jax.random.fold_in(rng, 2), number_of)[rank].astype(jnp.int32)


def centred(stream_key, extent, deviation, reach, cuts=(), dtype=jnp.bfloat16):
    entries = deviation * jax.random.normal(stream_key, extent, jnp.float32)
    if cuts:
        entries = entries * level_of(stream_key, extent, cuts, -0.22, 0.18)
    return jnp.clip(entries, -reach, reach).astype(dtype)


def setup_inputs(seed: int = 0) -> dict:
    arg_keys = jax.random.split(jax.random.key(seed), 10)
    attn_heads = centred(arg_keys[0], (TOKENS, D), 1.0, 6.0, ((0, 32), (1, 4)))
    out_proj = centred(arg_keys[1], (D, D), D ** -0.5, 0.0625, ((0, 4), (1, 32)))
    low_tap = centred(arg_keys[2], (TOKENS, D), 1.0, 6.0, ((0, 4), (1, 32)))
    mid_tap = centred(arg_keys[3], (TOKENS, D), 1.0, 6.0, ((0, 4), (1, 32)))
    join_weight = centred(arg_keys[4], (3, D, D), (3 * D) ** -0.5, 0.0390625, ((1, 32), (2, 4)))
    norm_gain = jnp.clip(1.0 + 0.1 * jax.random.normal(arg_keys[5], (D,), jnp.float32), 0.5, 1.5)
    head_weight = draw_head_weight(jax.random.fold_in(arg_keys[9], 71), 0)
    targets = set_ends(skewed_ids(arg_keys[7], (TOKENS,), VOCAB, 2), jax.random.fold_in(arg_keys[7], 3), 0, VOCAB - 1).astype(jnp.int32)
    loss_mask = set_ends((jax.random.randint(arg_keys[8], (TOKENS,), 0, 4) < 3).astype(jnp.int32), jax.random.fold_in(arg_keys[8], 1), 0, 1)
    return dict(attn_heads=attn_heads, out_proj=out_proj, low_tap=low_tap, mid_tap=mid_tap, join_weight=join_weight, norm_gain=norm_gain, head_weight=head_weight, targets=targets, loss_mask=loss_mask)


def reference(attn_heads, out_proj, low_tap, mid_tap, join_weight, norm_gain, head_weight, targets, loss_mask):
    projected = jnp.dot(attn_heads, out_proj, preferred_element_type=jnp.float32)
    high_tap = (mid_tap.astype(jnp.float32) + projected).astype(jnp.bfloat16)
    taps = jnp.concatenate([low_tap, mid_tap, high_tap], axis=1)
    joined = jnp.dot(taps, join_weight.reshape(3 * D, D), preferred_element_type=jnp.float32)
    scale = jax.lax.rsqrt(lax.optimization_barrier(jnp.mean(joined * joined, axis=1)) + 1e-05)
    draft_hidden = (joined * scale[:, None] * norm_gain[None, :]).astype(jnp.bfloat16)
    logits = jnp.dot(draft_hidden, head_weight, preferred_element_type=jnp.float32)
    top = lax.optimization_barrier(jnp.max(logits, axis=1))
    total = lax.optimization_barrier(jnp.sum(jnp.exp(logits - top[:, None]), axis=1))
    picked = jnp.take_along_axis(logits, targets[:, None].astype(jnp.int32), axis=1)[:, 0]
    row_loss = loss_mask.astype(jnp.float32) * (top + jnp.log(total) - picked)
    return (draft_hidden, row_loss)
```

```python
import functools

import jax
import jax.numpy as jnp
from jax import lax
from jax.experimental import pallas as pl
from jax.experimental.pallas import tpu as pltpu
from jax.sharding import PartitionSpec as P

MESH = pl.DeviceIdType.MESH
C = 4
F32 = jnp.float32
BF16 = jnp.bfloat16
WIDTH = 8192

TIMES = {
    "a_own": (0.0, 4.0),
    "a_line": (3.0, 4.0),
    "a_near": (7.0, 4.5),
    "mm1": (11.0, 4.5),
    "high": (15.0, 5.0),
    "mm2": (19.0, 8.0),
    "far": (24.0, 8.0),
    "near": (27.0, 8.0),
    "join": (30.0, 8.0),
    "norm": (33.0, 8.0),
    "h_line": (36.0, 8.0),
    "h_near": (40.0, 8.0),
    "mm3": (44.0, 8.5),
    "loss": (56.0, 10.0),
    "fold_a": (59.0, 10.0),
    "fold_b": (62.0, 10.0),
    "put": (64.0, 10.0),
}

SEMS = {
    "own": (C,),
    "weights": (3,),
    "tap_own": (2,),
}
PAIRS = {
    "sib": (3,),
    "tap": (2, 2, 4),
    "a1": (C, 3),
    "a2": (C, 2, 4),
    "a3": (C, 4),
    "h1": (C, 3),
    "h2": (C, 2, 4),
    "h3": (C, 4),
    "zr": (C, 3),
    "zg": (C, 3),
    "rf": (C, 2),
    "rn": (C, 2, 2),
    "ra": (C, 3),
    "sq": (C, 3),
    "lz": (C, 3),
    "fa": (C, 3),
    "fb": (C, 3),
    "fc": (C,),
}
BUFS = {
    "G1": ((C, 4, 4, 16, 2048), BF16),
    "G2": ((C, 4, 4, 16, 2048), BF16),
    "OPW": ((2, 2048, 256), BF16),
    "JW": ((3, 512, 2048), BF16),
    "HW": ((2, 2048, 1000), BF16),
    "T": ((3, 4, 4, C, 16, 512), BF16),
    "P1": ((C, 4, 4, 16, 512), BF16),
    "RH": ((C, 3, 4, 16, 512), BF16),
    "P2": ((C, 4, 4, 16, 2048), BF16),
    "RF": ((C, 2, 2, 16, 2048), BF16),
    "RN": ((C, 2, 4, 16, 2048), BF16),
    "Q": ((C, 4, 16, 2048), BF16),
    "RA": ((C, 3, 16, 2048), BF16),
    "J": ((C, 16, 2048), F32),
    "SQ": ((C, 4, 16, 128), F32),
    "P3": ((C, 4, 4, 2, 16, 1000), BF16),
    "LZ": ((C, 3, 4, 2, 16, 1000), BF16),
    "FA": ((C, 4, 64, 128), F32),
    "FB": ((C, 4, 64, 128), F32),
    "FC": ((C, 2, 4, 16, 128), F32),
}


def kernel(attn, oproj, low, mid, joinw, headw, gain, tgt, msk, out, loss_out, *scratch):
    names = list(BUFS) + list(SEMS) + [n + s for n in PAIRS for s in ("_s", "_r")]
    S = dict(zip(names, scratch))
    G1, G2, OPW, JW, HW, T = (S[n] for n in ("G1", "G2", "OPW", "JW", "HW", "T"))
    P1, RH, P2, RF, RN, Q, RA, J = (S[n] for n in ("P1", "RH", "P2", "RF", "RN", "Q", "RA", "J"))
    SQ, P3, LZ, FA, FB, FC = (S[n] for n in ("SQ", "P3", "LZ", "FA", "FB", "FC"))

    dp, z, g = lax.axis_index("dp"), lax.axis_index("tensor"), lax.axis_index("group")
    x, c = dp // 2, dp % 2
    a = (1 - c) * x + c * g
    b = (1 - c) * g + c * x

    def place(x, c, z, g):
        return (x * 2 + c, z, g)

    def along_a(j):
        return place((x + (1 - c) * j) % 4, c, z, (g + c * j) % 4)

    def along_b(j):
        return place((x + c * j) % 4, c, z, (g + (1 - c) * j) % 4)

    def along_z(j, e=0):
        return place(x, (c + e) % 2, (z + j) % 4, g)

    sib = along_z(0, 1)
    sent = []

    def send(name, index, src, dst, device):
        copy = pltpu.make_async_remote_copy(
            src_ref=src, dst_ref=dst, send_sem=S[name + "_s"].at[index],
            recv_sem=S[name + "_r"].at[index], device_id=device, device_id_type=MESH,
        )
        copy.start()
        sent.append(copy)

    def arrived(name, index, slot):
        pltpu.make_async_remote_copy(
            src_ref=slot, dst_ref=slot, send_sem=S[name + "_s"].at[index],
            recv_sem=S[name + "_r"].at[index], device_id=sib, device_id_type=MESH,
        ).wait_recv()

    barrier = pltpu.get_barrier_semaphore()
    partners = [along_a(j) for j in (1, 2, 3)] + [along_b(j) for j in (1, 2, 3)]
    partners += [along_z(j, e) for e in (0, 1) for j in range(4) if (j, e) != (0, 0)]
    for device in partners:
        pl.semaphore_signal(barrier, inc=1, device_id=device, device_id_type=MESH)

    local = {}

    def local_copy(key, src, dst, sem):
        local[key] = pltpu.make_async_copy(src, dst, sem)
        local[key].start()

    cols = pl.ds(pl.multiple_of(c * 256, 256), 256)
    local_copy("op", oproj, OPW.at[c], S["weights"].at[0])
    local_copy("jw", joinw, JW.at[:, cols], S["weights"].at[1])
    local_copy("hw", headw, HW.at[c], S["weights"].at[2])
    for t, tap in enumerate((low, mid)):
        local_copy(("tap", t), tap.at[c], T.at[t, z, :, :, :, cols], S["tap_own"].at[t])
    for k in range(C):
        local_copy(("own", k), attn.at[k], G1.at[k, b, a], S["own"].at[k])
    pl.semaphore_wait(barrier, len(partners))

    def gather_own(n, G, k, own):
        for j in (1, 3, 2):
            send(n + "1", (k, j - 1), own, G.at[k, b, a], along_a(j))
        send(n + "2", (k, 0, 0), own, G.at[k, b, a], along_b(1))
        send(n + "2", (k, 1, 0), own, G.at[k, b, a], along_b(3))

    def gather_line(n, G, k):
        for j in (1, 3, 2):
            slot = G.at[k, b, (a + 4 - j) % 4]
            arrived(n + "1", (k, j - 1), slot)
            send(n + "2", (k, 0, j), slot, slot, along_b(1))
            send(n + "2", (k, 1, j), slot, slot, along_b(3))

    def gather_near(n, G, k):
        for j in (0, 1, 3, 2):
            for d, way in ((0, 1), (1, 3)):
                slot = G.at[k, (b + 4 - way) % 4, (a + 4 - j) % 4]
                arrived(n + "2", (k, d, j), slot)
                if (j in (0, 2)) == (d == 0):
                    send(n + "3", (k, j), slot, slot, along_b(way))

    def gather_far(n, G, k):
        for j in (0, 1, 3, 2):
            arrived(n + "3", (k, j), G.at[k, (b + 2) % 4, (a + 4 - j) % 4])

    def a_own(k):
        gather_own("a", G1, k, attn.at[k])

    def a_line(k):
        gather_line("a", G1, k)

    def a_near(k):
        gather_near("a", G1, k)

    def mm1(k):
        local[("own", k)].wait()
        if k == 0:
            local["op"].wait()
            arrived("sib", (0,), OPW.at[1 - c])
        gather_far("a", G1, k)
        rows = G1[k].reshape(256, 2048)
        for p in range(2):
            part = jnp.dot(rows, OPW[p], preferred_element_type=F32).astype(BF16)
            part = part.reshape(4, 4, 16, 256)
            for i in range(4):
                for h in range(4):
                    P1[k, (1 - c) * h + c * i, (1 - c) * i + c * h, :, p * 256:(p + 1) * 256] = part[i, h]
        for j in (1, 3, 2):
            to = (z + j) % 4
            send("zr", (k, j - 1), P1.at[k, to], RH.at[k, j - 1], along_z(j))

    def high(k):
        if k == 0:
            for t in range(2):
                local[("tap", t)].wait()
                for e in range(2):
                    for j in range(4):
                        if (j, e) != (0, 0):
                            from_cols = pl.ds(pl.multiple_of(((c + e) % 2) * 256, 256), 256)
                            arrived("tap", (t, e, j), T.at[t, (z + 4 - j) % 4, :, :, :, from_cols])
        for j in (1, 3, 2):
            arrived("zr", (k, j - 1), RH.at[k, j - 1])
        total = P1[k, z].astype(F32)
        for j in range(3):
            total += RH[k, j].astype(F32)
        T[2, z, :, k] = (T[1, z, :, k].astype(F32) + total).astype(BF16)
        for j in (1, 3, 2):
            slot = T.at[2, z, :, k]
            send("zg", (k, j - 1), slot, slot, along_z(j))

    def mm2(k):
        if k == 0:
            local["jw"].wait()
            other = pl.ds(pl.multiple_of((1 - c) * 256, 256), 256)
            arrived("sib", (1,), JW.at[:, other])
        for j in (1, 3, 2):
            arrived("zg", (k, j - 1), T.at[2, (z + 4 - j) % 4, :, k])

        @pl.loop(0, 4)
        def _(n):
            wide = pl.ds(pl.multiple_of(n * 512, 512), 512)
            acc = jnp.zeros((256, 512), F32)
            for t in range(3):
                acc += jnp.dot(T[t, :, :, k].reshape(256, 512), JW[t, :, wide], preferred_element_type=F32)
            acc = acc.astype(BF16).reshape(4, 4, 16, 512)
            for i in range(4):
                for h in range(4):
                    P2[k, (1 - c) * h + c * i, (1 - c) * i + c * h, :, wide] = acc[i, h]

        far, up, down = (b + 2) % 4, (b + 1) % 4, (b + 3) % 4
        send("rf", (k, 0), P2.at[k, far, 0:2], RF.at[k, 0], along_b(1))
        send("rf", (k, 1), P2.at[k, far, 2:4], RF.at[k, 1], along_b(3))
        send("rn", (k, 0, 1), P2.at[k, up, 2:4], RN.at[k, 0, 2:4], along_b(1))
        send("rn", (k, 1, 0), P2.at[k, down, 0:2], RN.at[k, 1, 0:2], along_b(3))

    def far(k):
        for d, way, lo in ((0, 1, 0), (1, 3, 2)):
            to = (b + way) % 4
            arrived("rf", (k, d), RF.at[k, d])
            both = P2[k, to, lo:lo + 2].astype(F32) + RF[k, d].astype(F32)
            P2[k, to, lo:lo + 2] = both.astype(BF16)
            send("rn", (k, d, lo // 2), P2.at[k, to, lo:lo + 2], RN.at[k, d, lo:lo + 2], along_b(way))

    def near(k):
        for d in range(2):
            for h in range(2):
                arrived("rn", (k, d, h), RN.at[k, d, 2 * h:2 * h + 2])
        for h in range(4):
            total = P2[k, b, h].astype(F32) + RN[k, 0, h].astype(F32) + RN[k, 1, h].astype(F32)
            Q[k, h] = total.astype(BF16)
        for j in (1, 3, 2):
            send("ra", (k, j - 1), Q.at[k, (a + j) % 4], RA.at[k, j - 1], along_a(j))

    def join(k):
        for j in (1, 3, 2):
            arrived("ra", (k, j - 1), RA.at[k, j - 1])
        total = P2[k, b, a].astype(F32) + RN[k, 0, a].astype(F32) + RN[k, 1, a].astype(F32)
        for j in range(3):
            total += RA[k, j].astype(F32)
        J[k] = total
        SQ[k, 3] = jnp.broadcast_to(jnp.sum(total * total, axis=1, keepdims=True), (16, 128))
        for j in (1, 3, 2):
            send("sq", (k, j - 1), SQ.at[k, 3], SQ.at[k, j - 1], along_z(j))

    def norm(k):
        for j in (1, 3, 2):
            arrived("sq", (k, j - 1), SQ.at[k, j - 1])
        squares = SQ[k, 0] + SQ[k, 1] + SQ[k, 2] + SQ[k, 3]
        scale = lax.rsqrt(squares[:, 0:1] / WIDTH + 1e-05)
        hidden = (J[k] * scale * gain[...]).astype(BF16)
        G2[k, b, a] = hidden
        out[k] = hidden
        gather_own("h", G2, k, G2.at[k, b, a])

    def h_line(k):
        gather_line("h", G2, k)

    def h_near(k):
        gather_near("h", G2, k)

    def mm3(k):
        if k == 0:
            local["hw"].wait()
            arrived("sib", (2,), HW.at[1 - c])
        gather_far("h", G2, k)
        rows = G2[k].reshape(256, 2048)
        for p in range(2):
            for lo, hi in ((0, 256), (256, 512), (512, 768), (768, 1000)):
                part = jnp.dot(rows, HW[p, :, lo:hi], preferred_element_type=F32).astype(BF16)
                part = part.reshape(4, 4, 16, hi - lo)
                for i in range(4):
                    for h in range(4):
                        P3[k, (1 - c) * h + c * i, (1 - c) * i + c * h, p, :, lo:hi] = part[i, h]
        for j in (1, 3, 2):
            send("lz", (k, j - 1), P3.at[k, (z + j) % 4], LZ.at[k, j - 1], along_z(j))

    lane = lax.broadcasted_iota(jnp.int32, (64, 128), 1)

    def packed(top, total, picked):
        return jnp.where(lane == 0, top, jnp.where(lane == 1, total, picked))

    def loss(k):
        for j in (1, 3, 2):
            arrived("lz", (k, j - 1), LZ.at[k, j - 1])
        ids = tgt[c, :, k].reshape(64, 1)
        logits, picked = [], jnp.zeros((64, 1), F32)
        for p in range(2):
            total = P3[k, z, :, p].astype(F32)
            for j in range(3):
                total += LZ[k, j, :, p].astype(F32)
            total = total.reshape(64, 1000)
            here = lax.broadcasted_iota(jnp.int32, (64, 1000), 1) + ((x * 2 + p) * 4 + g) * 1000
            picked += jnp.sum(jnp.where(here == ids, total, 0.0), axis=1, keepdims=True)
            logits.append(total)
        top = jnp.maximum(*(jnp.max(v, axis=1, keepdims=True) for v in logits))
        total = sum(jnp.sum(jnp.exp(v - top), axis=1, keepdims=True) for v in logits)
        FA[k, 3] = packed(top, total, picked)
        for j in (1, 3, 2):
            send("fa", (k, j - 1), FA.at[k, 3], FA.at[k, j - 1], along_a(j))

    def merged(F, k):
        parts = [F[k, j] for j in range(4)]
        tops = [v[:, 0:1] for v in parts]
        top = jnp.maximum(jnp.maximum(tops[0], tops[1]), jnp.maximum(tops[2], tops[3]))
        total = sum(v[:, 1:2] * jnp.exp(t - top) for v, t in zip(parts, tops))
        picked = sum(v[:, 2:3] for v in parts)
        return top, total, picked

    def fold_a(k):
        for j in (1, 3, 2):
            arrived("fa", (k, j - 1), FA.at[k, j - 1])
        FB[k, 3] = packed(*merged(FA, k))
        for j in (1, 3, 2):
            send("fb", (k, j - 1), FB.at[k, 3], FB.at[k, j - 1], along_b(j))

    def fold_b(k):
        for j in (1, 3, 2):
            arrived("fb", (k, j - 1), FB.at[k, j - 1])
        top, total, picked = merged(FB, k)
        mask = msk[c, :, k].reshape(64, 1).astype(F32)
        value = (mask * (top + jnp.log(total) - picked)).reshape(4, 16, 1)
        loss_out[c, :, k] = value
        FC[k, 0] = jnp.broadcast_to(value, (4, 16, 128))
        send("fc", (k,), FC.at[k, 0], FC.at[k, 1], sib)

    def put(k):
        arrived("fc", (k,), FC.at[k, 1])
        loss_out[1 - c, :, k] = FC[k, 1][:, :, 0:1]

    def weights(k):
        send("sib", (0,), oproj, OPW.at[c], sib)
        for j in (1, 3, 2, 0):
            for e in range(2):
                if (j, e) != (0, 0):
                    for t, tap in enumerate((low, mid)):
                        send("tap", (t, e, j), tap.at[(c + e) % 2], T.at[t, z, :, :, :, cols], along_z(j, e))
        send("sib", (1,), joinw, JW.at[:, cols], sib)
        send("sib", (2,), headw, HW.at[c], sib)

    fns = dict(
        a_own=a_own, a_line=a_line, a_near=a_near, mm1=mm1, high=high, mm2=mm2, far=far, near=near, join=join,
        norm=norm, h_line=h_line, h_near=h_near, mm3=mm3, loss=loss, fold_a=fold_a, fold_b=fold_b, put=put,
    )
    order = [(at + step * k, i, k, fns[n]) for i, (n, (at, step)) in enumerate(TIMES.items()) for k in range(C)]
    order.append((0.5, 0, 0, weights))
    for _, _, k, fn in sorted(order, key=lambda v: v[:3]):
        fn(k)
    for copy in sent:
        copy.wait_send()


def on_device(attn_heads, out_proj, low_tap, mid_tap, join_weight, norm_gain, head_weight, targets, loss_mask):
    anywhere = pl.BlockSpec(memory_space=pl.ANY)
    vmem = pl.BlockSpec(memory_space=pltpu.VMEM)
    sems = [pltpu.SemaphoreType.DMA(s) for s in SEMS.values()]
    sems += [pltpu.SemaphoreType.DMA(s) for s in PAIRS.values() for _ in range(2)]
    hidden, loss = pl.pallas_call(
        kernel,
        name="draft_head",
        out_shape=(
            jax.ShapeDtypeStruct((C, 16, 2048), BF16),
            jax.ShapeDtypeStruct((2, 4, C, 16, 1), F32),
        ),
        in_specs=[anywhere] * 6 + [vmem] * 3,
        out_specs=(vmem, vmem),
        scratch_shapes=[pltpu.VMEM(*s) for s in BUFS.values()] + sems,
        compiler_params=pltpu.CompilerParams(collective_id=0, has_side_effects=True, vmem_limit_bytes=60 << 20),
    )(
        attn_heads.reshape(C, 16, 2048),
        out_proj,
        low_tap.reshape(2, 4, C, 16, 256),
        mid_tap.reshape(2, 4, C, 16, 256),
        join_weight,
        head_weight,
        norm_gain.reshape(1, 2048),
        targets.reshape(2, 4, C, 16, 1),
        loss_mask.reshape(2, 4, C, 16, 1),
    )
    return hidden.reshape(64, 2048), loss.reshape(512)


def solution(mesh):
    in_specs = (
        P(("dp", "group"), "tensor"),
        P("tensor", ("dp", "group")),
        P("tensor", ("dp", "group")),
        P("tensor", ("dp", "group")),
        P(None, ("dp", "group"), "tensor"),
        P("tensor"),
        P("tensor", ("dp", "group")),
        P("tensor"),
        P("tensor"),
    )
    out_specs = (P(("dp", "group"), "tensor"), P("tensor"))
    return jax.shard_map(
        on_device, mesh=mesh, in_specs=in_specs, out_specs=out_specs, check_vma=False
    )
```

```python
import functools

import jax
import jax.numpy as jnp
from jax import lax
from jax.experimental import pallas as pl
from jax.experimental.pallas import tpu as pltpu
from jax.sharding import PartitionSpec as P

MESH = pl.DeviceIdType.MESH
C = 4
F32 = jnp.float32
BF16 = jnp.bfloat16
WIDTH = 8192

TIMES = {
    "taps": (0.2, 6.0),
    "a_own": (0.0, 0.02),
    "a_line": (3.0, 2.0),
    "a_far_line": (4.0, 2.0),
    "a_near0": (5.0, 2.0),
    "a_near": (6.0, 2.0),
    "a_near2": (7.0, 2.0),
    "mm1": (10.0, 4.0),
    "high": (14.0, 4.0),
    "mm2": (18.0, 6.0),
    "far": (22.0, 6.0),
    "near": (25.0, 6.0),
    "join": (28.0, 6.0),
    "h_line": (31.0, 6.0),
    "h_far_line": (32.0, 6.0),
    "h_near0": (33.0, 6.0),
    "h_near": (34.0, 6.0),
    "h_near2": (36.0, 6.0),
    "norm": (37.0, 6.0),
    "mm3": (39.0, 8.0),
    "loss": (50.0, 8.0),
}

SEMS = {
    "own": (C,),
    "weights": (3,),
    "tap_own": (C, 2),
}
PAIRS = {
    "sib": (3,),
    "tap": (C, 2, 2, 4),
    "a1": (C, 3),
    "a2": (C, 2, 4),
    "a3": (C, 4),
    "h1": (C, 3),
    "h2": (C, 2, 4),
    "h3": (C, 4),
    "zr": (C, 3),
    "zg": (C, 3),
    "rf": (C, 2),
    "rn": (C, 2, 2),
    "ra": (C, 3),
    "sq": (C, 3),
    "lz": (C, 3, 2),
    "ss": (C, 3),
    "st": (8, 4),
}
BUFS = {
    "G1": ((C, 4, 4, 16, 2048), BF16),
    "G2": ((C, 4, 4, 16, 2048), BF16),
    "OPW": ((2, 2048, 256), BF16),
    "JW": ((3, 512, 2048), BF16),
    "HW": ((2, 1000, 2048), BF16),
    "T": ((3, 4, 4, C, 16, 512), BF16),
    "P1": ((C, 4, 4, 16, 512), BF16),
    "RH": ((C, 3, 4, 16, 512), BF16),
    "P2": ((C, 4, 4, 16, 2048), BF16),
    "RF": ((C, 2, 2, 16, 2048), BF16),
    "RN": ((C, 2, 4, 16, 2048), BF16),
    "Q": ((C, 4, 16, 2048), BF16),
    "RA": ((C, 3, 16, 2048), BF16),
    "J": ((C, 16, 2048), F32),
    "SQ": ((C, 4, 16, 128), F32),
    "H": ((256, 2048), BF16),
    "SS": ((C, 4, 4, 16, 128), F32),
    "SZ": ((C, 3, 4, 16, 128), F32),
    "P3": ((C, 4, 2, 4, 16, 1000), BF16),
    "LZ": ((C, 3, 2, 4, 16, 1000), BF16),
    "STATS": ((4, C, 16, 128), F32),
    "ST": ((8, 4, 2, 8, 128), F32),
    "IDS": ((4, C, 16, 128), jnp.int32),
}


def kernel(attn, oproj, low, mid, joinw, headw, gain, tgt, msk, out, loss_out, *scratch):
    names = list(BUFS) + list(SEMS) + [n + s for n in PAIRS for s in ("_s", "_r")]
    S = dict(zip(names, scratch))
    G1, G2, OPW, JW, HW, T = (S[n] for n in ("G1", "G2", "OPW", "JW", "HW", "T"))
    P1, RH, P2, RF, RN, Q, RA, J = (S[n] for n in ("P1", "RH", "P2", "RF", "RN", "Q", "RA", "J"))
    SQ, P3, LZ, H, SS, SZ = (S[n] for n in ("SQ", "P3", "LZ", "H", "SS", "SZ"))
    IDS, STATS, ST = (S[n] for n in ("IDS", "STATS", "ST"))

    dp, z, g = lax.axis_index("dp"), lax.axis_index("tensor"), lax.axis_index("group")
    x, c = dp // 2, dp % 2
    a = (1 - c) * x + c * g
    b = (1 - c) * g + c * x

    def place(x, c, z, g):
        return (x * 2 + c, z, g)

    def along_a(j):
        return place((x + (1 - c) * j) % 4, c, z, (g + c * j) % 4)

    def along_b(j):
        return place((x + c * j) % 4, c, z, (g + (1 - c) * j) % 4)

    def along_z(j, e=0):
        return place(x, (c + e) % 2, (z + j) % 4, g)

    sib = along_z(0, 1)
    sent = []

    def send(name, index, src, dst, device):
        copy = pltpu.make_async_remote_copy(
            src_ref=src, dst_ref=dst, send_sem=S[name + "_s"].at[index],
            recv_sem=S[name + "_r"].at[index], device_id=device, device_id_type=MESH,
        )
        copy.start()
        sent.append(copy)

    def arrived(name, index, slot):
        pltpu.make_async_remote_copy(
            src_ref=slot, dst_ref=slot, send_sem=S[name + "_s"].at[index],
            recv_sem=S[name + "_r"].at[index], device_id=sib, device_id_type=MESH,
        ).wait_recv()

    barrier = pltpu.get_barrier_semaphore()
    plane = [(i, j) for i in range(8) for j in range(4) if (i, j) != (0, 0)]

    def in_plane(i, j):
        return ((dp + i) % 8, z, (g + j) % 4)

    partners = [in_plane(i, j) for i, j in plane]
    partners += [along_z(j, e) for e in (0, 1) for j in (1, 2, 3)]
    for device in partners:
        pl.semaphore_signal(barrier, inc=1, device_id=device, device_id_type=MESH)

    local = {}

    def local_copy(key, src, dst, sem):
        local[key] = pltpu.make_async_copy(src, dst, sem)
        local[key].start()

    cols = pl.ds(pl.multiple_of(c * 256, 256), 256)
    local_copy("op", oproj, OPW.at[c], S["weights"].at[0])
    local_copy("jw", joinw, JW.at[:, cols], S["weights"].at[1])
    local_copy("hw", headw, HW.at[c], S["weights"].at[2])
    for k in range(C):
        for t, tap in enumerate((low, mid)):
            local_copy(("tap", k, t), tap.at[c, :, k], T.at[t, z, :, k, :, cols], S["tap_own"].at[k, t])
        local_copy(("own", k), attn.at[k], G1.at[k, b, a], S["own"].at[k])
    for h in range(2):
        row = pl.ds(2 * c + h, 1)
        IDS[2 * h:2 * h + 2] = jnp.transpose(jnp.broadcast_to(tgt[row], (128, 128))).reshape(2, C, 16, 128)
    pl.semaphore_wait(barrier, len(partners))

    waited = set()

    def ready(name):
        if name in waited:
            return
        waited.add(name)
        other = pl.ds(pl.multiple_of((1 - c) * 256, 256), 256)
        slots = {"op": OPW.at[1 - c], "jw": JW.at[:, other], "hw": HW.at[1 - c]}
        local[name].wait()
        arrived("sib", (list(slots).index(name),), slots[name])

    def gather_own(n, G, k, own):
        for j in (1, 3, 2):
            send(n + "1", (k, j - 1), own, G.at[k, b, a], along_a(j))
        send(n + "2", (k, 0, 0), own, G.at[k, b, a], along_b(1))
        send(n + "2", (k, 1, 0), own, G.at[k, b, a], along_b(3))

    def gather_line(n, G, k, steps):
        for j in steps:
            slot = G.at[k, b, (a + 4 - j) % 4]
            arrived(n + "1", (k, j - 1), slot)
            send(n + "2", (k, 0, j), slot, slot, along_b(1))
            send(n + "2", (k, 1, j), slot, slot, along_b(3))

    def gather_near(n, G, k, steps):
        for j in steps:
            for d, way in ((0, 1), (1, 3)):
                slot = G.at[k, (b + 4 - way) % 4, (a + 4 - j) % 4]
                arrived(n + "2", (k, d, j), slot)
                if (j in (0, 2)) == (d == 0):
                    send(n + "3", (k, j), slot, slot, along_b(way))

    def gather_far(n, G, k):
        for j in (0, 1, 3, 2):
            arrived(n + "3", (k, j), G.at[k, (b + 2) % 4, (a + 4 - j) % 4])

    def a_own(k):
        gather_own("a", G1, k, attn.at[k])

    def mm1(k):
        local[("own", k)].wait()
        ready("op")
        gather_far("a", G1, k)
        rows = G1[k].reshape(256, 2048)
        for p in range(2):
            part = jnp.dot(rows, OPW[p], preferred_element_type=F32).astype(BF16)
            part = part.reshape(4, 4, 16, 256)
            for i in range(4):
                for h in range(4):
                    P1[k, (1 - c) * h + c * i, (1 - c) * i + c * h, :, p * 256:(p + 1) * 256] = part[i, h]
        for j in (1, 3, 2):
            to = (z + j) % 4
            send("zr", (k, j - 1), P1.at[k, to], RH.at[k, j - 1], along_z(j))

    def high(k):
        for t in range(2):
            local[("tap", k, t)].wait()
            for j, e in z_partners:
                from_cols = pl.ds(pl.multiple_of(((c + e) % 2) * 256, 256), 256)
                arrived("tap", (k, t, e, j), T.at[t, (z + 4 - j) % 4, :, k, :, from_cols])
        for j in (1, 3, 2):
            arrived("zr", (k, j - 1), RH.at[k, j - 1])
        total = P1[k, z].astype(F32)
        for j in range(3):
            total += RH[k, j].astype(F32)
        T[2, z, :, k] = (T[1, z, :, k].astype(F32) + total).astype(BF16)
        for j in (1, 3, 2):
            slot = T.at[2, z, :, k]
            send("zg", (k, j - 1), slot, slot, along_z(j))

    def mm2(k):
        ready("jw")
        for j in (1, 3, 2):
            arrived("zg", (k, j - 1), T.at[2, (z + 4 - j) % 4, :, k])

        @pl.loop(0, 4)
        def _(n):
            wide = pl.ds(pl.multiple_of(n * 512, 512), 512)
            acc = jnp.zeros((256, 512), F32)
            for t in range(3):
                acc += jnp.dot(T[t, :, :, k].reshape(256, 512), JW[t, :, wide], preferred_element_type=F32)
            acc = acc.astype(BF16).reshape(4, 4, 16, 512)
            for i in range(4):
                for h in range(4):
                    P2[k, (1 - c) * h + c * i, (1 - c) * i + c * h, :, wide] = acc[i, h]

        far, up, down = (b + 2) % 4, (b + 1) % 4, (b + 3) % 4
        send("rf", (k, 0), P2.at[k, far, 0:2], RF.at[k, 0], along_b(1))
        send("rf", (k, 1), P2.at[k, far, 2:4], RF.at[k, 1], along_b(3))
        send("rn", (k, 0, 1), P2.at[k, up, 2:4], RN.at[k, 0, 2:4], along_b(1))
        send("rn", (k, 1, 0), P2.at[k, down, 0:2], RN.at[k, 1, 0:2], along_b(3))

    def far(k):
        for d, way, lo in ((0, 1, 0), (1, 3, 2)):
            to = (b + way) % 4
            arrived("rf", (k, d), RF.at[k, d])
            both = P2[k, to, lo:lo + 2].astype(F32) + RF[k, d].astype(F32)
            P2[k, to, lo:lo + 2] = both.astype(BF16)
            send("rn", (k, d, lo // 2), P2.at[k, to, lo:lo + 2], RN.at[k, d, lo:lo + 2], along_b(way))

    def near(k):
        for d in range(2):
            for h in range(2):
                arrived("rn", (k, d, h), RN.at[k, d, 2 * h:2 * h + 2])
        for h in range(4):
            total = P2[k, b, h].astype(F32) + RN[k, 0, h].astype(F32) + RN[k, 1, h].astype(F32)
            Q[k, h] = total.astype(BF16)
        for j in (1, 3, 2):
            send("ra", (k, j - 1), Q.at[k, (a + j) % 4], RA.at[k, j - 1], along_a(j))

    def join(k):
        for j in (1, 3, 2):
            arrived("ra", (k, j - 1), RA.at[k, j - 1])
        total = P2[k, b, a].astype(F32) + RN[k, 0, a].astype(F32) + RN[k, 1, a].astype(F32)
        for j in range(3):
            total += RA[k, j].astype(F32)
        J[k] = total
        SQ[k, 3] = jnp.broadcast_to(jnp.sum(total * total, axis=1, keepdims=True), (16, 128))
        G2[k, b, a] = total.astype(BF16)
        gather_own("h", G2, k, G2.at[k, b, a])
        for j in (1, 3, 2):
            send("sq", (k, j - 1), SQ.at[k, 3], SQ.at[k, j - 1], along_z(j))

    def norm(k):
        for j in (1, 3, 2):
            arrived("sq", (k, j - 1), SQ.at[k, j - 1])
        squares = SQ[k, 0] + SQ[k, 1] + SQ[k, 2] + SQ[k, 3]
        scale = lax.rsqrt(squares[:, 0:1] / WIDTH + 1e-05)
        out[k] = (J[k] * scale * gain[...]).astype(BF16)

    def mm3(k):
        ready("hw")
        gather_far("h", G2, k)
        joined = G2[k].reshape(256, 2048).astype(F32)
        H[...] = (joined * gain[...]).astype(BF16)
        squares = jnp.broadcast_to(jnp.sum(joined * joined, axis=1, keepdims=True), (256, 128))
        squares = squares.reshape(4, 4, 16, 128)
        for i in range(4):
            for h in range(4):
                SS[k, (1 - c) * h + c * i, (1 - c) * i + c * h] = squares[i, h]
        for j in (1, 3, 2):
            send("ss", (k, j - 1), SS.at[k, (z + j) % 4], SZ.at[k, j - 1], along_z(j))
        for p in range(2):
            for lo, hi in ((0, 256), (256, 512), (512, 768), (768, 1000)):
                part = lax.dot_general(
                    H[...], HW[p, lo:hi], (((1,), (1,)), ((), ())), preferred_element_type=F32
                ).astype(BF16)
                part = part.reshape(4, 4, 16, hi - lo)
                for i in range(4):
                    for h in range(4):
                        P3[k, (1 - c) * h + c * i, p, (1 - c) * i + c * h, :, lo:hi] = part[i, h]
            for j in (1, 3, 2):
                send("lz", (k, j - 1, p), P3.at[k, (z + j) % 4, p], LZ.at[k, j - 1, p], along_z(j))

    lane = lax.broadcasted_iota(jnp.int32, (64, 128), 1)

    def packed(top, total, picked):
        return jnp.where(lane == 0, top, jnp.where(lane == 1, total, picked))

    def loss(k):
        for j in (1, 3, 2):
            arrived("ss", (k, j - 1), SZ.at[k, j - 1])
        squares = SS[k, z] + SZ[k, 0] + SZ[k, 1] + SZ[k, 2]
        scale = lax.rsqrt(squares.reshape(64, 128)[:, 0:1] / WIDTH + 1e-05)
        ids = IDS[:, k].reshape(64, 128)[:, 0:1]
        logits, picked = [], jnp.zeros((64, 1), F32)
        for p in range(2):
            for j in (1, 3, 2):
                arrived("lz", (k, j - 1, p), LZ.at[k, j - 1, p])
            total = P3[k, z, p].astype(F32)
            for j in range(3):
                total += LZ[k, j, p].astype(F32)
            total = total.reshape(64, 1000) * scale
            here = lax.broadcasted_iota(jnp.int32, (64, 1000), 1) + ((x * 2 + p) * 4 + g) * 1000
            picked += jnp.sum(jnp.where(here == ids, total, 0.0), axis=1, keepdims=True)
            logits.append(total)
        top = jnp.maximum(*(jnp.max(v, axis=1, keepdims=True) for v in logits))
        total = sum(jnp.sum(jnp.exp(v - top), axis=1, keepdims=True) for v in logits)
        STATS[:, k] = packed(top, total, picked).reshape(4, 16, 128)

    def finish():
        for h in range(2):
            ST[0, 0, h] = jnp.transpose(STATS[2 * h:2 * h + 2].reshape(128, 128))[0:8]
        for i, j in plane:
            send("st", (i, j), ST.at[0, 0], ST.at[i, j], in_plane(i, j))
        for i, j in plane:
            arrived("st", (i, j), ST.at[i, j])
        for e in range(2):
            of = (c + e) % 2
            for h in range(2):
                parts = [ST[i, j, h] for i in range(e, 8, 2) for j in range(4)]
                top = functools.reduce(jnp.maximum, [v[0:1] for v in parts])
                total = sum(v[1:2] * jnp.exp(v[0:1] - top) for v in parts)
                picked = sum(v[2:3] for v in parts)
                row = pl.ds(2 * of + h, 1)
                loss_out[row] = msk[row].astype(F32) * (top + jnp.log(total) - picked)

    z_partners = [(0, 1), (2, 0), (2, 1), (1, 0), (1, 1), (3, 0), (3, 1)]

    def taps(k):
        for j, e in z_partners:
            for t, tap in enumerate((low, mid)):
                slot = T.at[t, z, :, k, :, cols]
                send("tap", (k, t, e, j), tap.at[(c + e) % 2, :, k], slot, along_z(j, e))
        if k == 0:
            send("sib", (0,), oproj, OPW.at[c], sib)
            send("sib", (1,), joinw, JW.at[:, cols], sib)
            send("sib", (2,), headw, HW.at[c], sib)

    fns = dict(
        taps=taps, a_own=a_own, mm1=mm1, high=high, mm2=mm2, far=far, near=near, join=join, norm=norm, mm3=mm3, loss=loss,
    )
    for n, G in (("a", G1), ("h", G2)):
        fns[n + "_line"] = functools.partial(gather_line, n, G, steps=(1, 3))
        fns[n + "_far_line"] = functools.partial(gather_line, n, G, steps=(2,))
        fns[n + "_near0"] = functools.partial(gather_near, n, G, steps=(0,))
        fns[n + "_near"] = functools.partial(gather_near, n, G, steps=(1, 3))
        fns[n + "_near2"] = functools.partial(gather_near, n, G, steps=(2,))
    order = [(at + step * k, i, n, k) for i, (n, (at, step)) in enumerate(TIMES.items()) for k in range(C)]
    for _, _, n, k in sorted(order):
        fns[n](k)
    finish()
    for copy in sent:
        copy.wait_send()


def on_device(attn_heads, out_proj, low_tap, mid_tap, join_weight, norm_gain, head_weight, targets, loss_mask):
    anywhere = pl.BlockSpec(memory_space=pl.ANY)
    vmem = pl.BlockSpec(memory_space=pltpu.VMEM)
    sems = [pltpu.SemaphoreType.DMA(s) for s in SEMS.values()]
    sems += [pltpu.SemaphoreType.DMA(s) for s in PAIRS.values() for _ in range(2)]
    hidden, loss = pl.pallas_call(
        kernel,
        name="draft_head",
        out_shape=(
            jax.ShapeDtypeStruct((C, 16, 2048), BF16),
            jax.ShapeDtypeStruct((4, 128), F32),
        ),
        in_specs=[anywhere] * 6 + [vmem] * 3,
        out_specs=(vmem, vmem),
        scratch_shapes=[pltpu.VMEM(*s) for s in BUFS.values()] + sems,
        compiler_params=pltpu.CompilerParams(collective_id=0, has_side_effects=True, vmem_limit_bytes=60 << 20),
    )(
        attn_heads.reshape(C, 16, 2048),
        out_proj,
        low_tap.reshape(2, 4, C, 16, 256),
        mid_tap.reshape(2, 4, C, 16, 256),
        join_weight,
        head_weight.T,
        norm_gain.reshape(1, 2048),
        targets.reshape(4, 128),
        loss_mask.reshape(4, 128),
    )
    return hidden.reshape(64, 2048), loss.reshape(512)


def solution(mesh):
    in_specs = (
        P(("dp", "group"), "tensor"),
        P("tensor", ("dp", "group")),
        P("tensor", ("dp", "group")),
        P("tensor", ("dp", "group")),
        P(None, ("dp", "group"), "tensor"),
        P("tensor"),
        P("tensor", ("dp", "group")),
        P("tensor"),
        P("tensor"),
    )
    out_specs = (P(("dp", "group"), "tensor"), P("tensor"))
    return jax.shard_map(
        on_device, mesh=mesh, in_specs=in_specs, out_specs=out_specs, check_vma=False
    )
```

```python
import functools

import jax
import jax.numpy as jnp
from jax import lax
from jax.experimental import pallas as pl
from jax.experimental.pallas import tpu as pltpu
from jax.sharding import PartitionSpec as P

MESH = pl.DeviceIdType.MESH
C = 4
F32 = jnp.float32
BF16 = jnp.bfloat16
WIDTH = 8192

ORDER = (
    ("taps_far", 0), ("a_own", 0), ("taps", 1), ("taps", 0), ("a_own", 1), ("a_line", 0), ("taps_far", 2),
    ("a_far_line", 0), ("a_line", 1), ("a_near0", 0), ("taps_far", 1), ("a_far_line", 1), ("a_near", 0),
    ("a_near2", 0), ("a_own", 2), ("a_near0", 1), ("a_near", 1), ("a_near2", 1), ("mm1", 0), ("a_own", 3),
    ("mm1", 1), ("a_line", 2), ("a_far_line", 2), ("a_line", 3), ("a_far_line", 3), ("high", 0),
    ("a_near0", 2), ("a_near", 2), ("a_near2", 2), ("a_near0", 3), ("high", 1), ("a_near", 3), ("mm1", 2),
    ("a_near2", 3), ("taps", 2), ("mm2", 0), ("mm2", 1), ("high", 2), ("far", 0), ("taps_far", 3), ("far", 1),
    ("mm1", 3), ("near", 0), ("taps", 3), ("near", 1), ("mm2", 2), ("join", 0), ("join", 1), ("high", 3),
    ("h_line", 0), ("h_far_line", 0), ("far", 2), ("h_line", 1), ("h_near0", 0), ("h_near", 0),
    ("h_near2", 0), ("h_far_line", 1), ("h_near0", 1), ("near", 2), ("mm2", 3), ("h_near", 1), ("mm3", 0),
    ("h_near2", 1), ("far", 3), ("norm", 0), ("join", 2), ("mm3", 1), ("near", 3), ("h_line", 2), ("norm", 2),
    ("h_far_line", 2), ("h_near0", 2), ("join", 3), ("lfar", 0), ("h_near", 2), ("h_near2", 2), ("norm", 1),
    ("lfar", 1), ("h_line", 3), ("h_far_line", 3), ("h_near0", 3), ("mm3", 2), ("h_near", 3), ("h_near2", 3),
    ("mm3", 3), ("lfar", 2), ("lfar", 3), ("loss", 1), ("loss", 0), ("norm", 3), ("loss", 2), ("loss", 3),
)

SEMS = {
    "own": (C,),
    "weights": (3,),
    "tap_own": (C, 2),
}
PAIRS = {
    "sib": (3,),
    "tap": (C, 2, 2, 4),
    "a1": (C, 3),
    "a2": (C, 2, 4),
    "a3": (C, 4),
    "h1": (C, 3),
    "h2": (C, 2, 4),
    "h3": (C, 4),
    "zr": (C, 3),
    "zg": (C, 3),
    "rf": (C, 2),
    "rn": (C, 2, 2),
    "ra": (C, 3),
    "sq": (C, 3),
    "lf": (C, 2),
    "ln": (C, 2, 2),
    "ss": (C, 3),
    "st": (8, 4),
}
BUFS = {
    "G1": ((C, 4, 4, 16, 2048), BF16),
    "G2": ((C, 4, 4, 16, 2048), BF16),
    "OPW": ((2, 2048, 256), BF16),
    "JW": ((3, 512, 2048), BF16),
    "HW": ((2, 1000, 2048), BF16),
    "T": ((3, 4, 4, C, 16, 512), BF16),
    "P1": ((C, 4, 4, 16, 512), BF16),
    "RH": ((C, 3, 4, 16, 512), BF16),
    "P2": ((C, 4, 4, 16, 2048), BF16),
    "RF": ((C, 2, 2, 16, 2048), BF16),
    "RN": ((C, 2, 4, 16, 2048), BF16),
    "Q": ((C, 4, 16, 2048), BF16),
    "RA": ((C, 3, 16, 2048), BF16),
    "J": ((C, 16, 2048), F32),
    "SQ": ((C, 4, 16, 128), F32),
    "H": ((256, 2048), BF16),
    "SS": ((C, 4, 4, 16, 128), F32),
    "SZ": ((C, 3, 4, 16, 128), F32),
    "P3": ((C, 4, 2, 4, 16, 1000), BF16),
    "LF": ((C, 2, 4, 16, 1000), BF16),
    "LN": ((C, 2, 2, 4, 16, 1000), BF16),
    "STATS": ((4, C, 16, 128), F32),
    "ST": ((8, 4, 2, 8, 128), F32),
    "IDS": ((4, C, 16, 128), jnp.int32),
}


def kernel(attn, oproj, low, mid, joinw, headw, gain, tgt, msk, out, loss_out, *scratch):
    names = list(BUFS) + list(SEMS) + [n + s for n in PAIRS for s in ("_s", "_r")]
    S = dict(zip(names, scratch))
    G1, G2, OPW, JW, HW, T = (S[n] for n in ("G1", "G2", "OPW", "JW", "HW", "T"))
    P1, RH, P2, RF, RN, Q, RA, J = (S[n] for n in ("P1", "RH", "P2", "RF", "RN", "Q", "RA", "J"))
    SQ, P3, LF, LN, H, SS, SZ = (S[n] for n in ("SQ", "P3", "LF", "LN", "H", "SS", "SZ"))
    IDS, STATS, ST = (S[n] for n in ("IDS", "STATS", "ST"))

    dp, z, g = lax.axis_index("dp"), lax.axis_index("tensor"), lax.axis_index("group")
    x, c = dp // 2, dp % 2
    a = (1 - c) * x + c * g
    b = (1 - c) * g + c * x

    def place(x, c, z, g):
        return (x * 2 + c, z, g)

    def along_a(j):
        return place((x + (1 - c) * j) % 4, c, z, (g + c * j) % 4)

    def along_b(j):
        return place((x + c * j) % 4, c, z, (g + (1 - c) * j) % 4)

    def along_z(j, e=0):
        return place(x, (c + e) % 2, (z + j) % 4, g)

    sib = along_z(0, 1)
    sent = []

    def send(name, index, src, dst, device):
        copy = pltpu.make_async_remote_copy(
            src_ref=src, dst_ref=dst, send_sem=S[name + "_s"].at[index],
            recv_sem=S[name + "_r"].at[index], device_id=device, device_id_type=MESH,
        )
        copy.start()
        sent.append(copy)

    def arrived(name, index, slot):
        pltpu.make_async_remote_copy(
            src_ref=slot, dst_ref=slot, send_sem=S[name + "_s"].at[index],
            recv_sem=S[name + "_r"].at[index], device_id=sib, device_id_type=MESH,
        ).wait_recv()

    barrier = pltpu.get_barrier_semaphore()
    plane = [(i, j) for i in range(8) for j in range(4) if (i, j) != (0, 0)]

    def in_plane(i, j):
        return ((dp + i) % 8, z, (g + j) % 4)

    partners = [in_plane(i, j) for i, j in plane]
    partners += [along_z(j, e) for e in (0, 1) for j in (1, 2, 3)]
    for device in partners:
        pl.semaphore_signal(barrier, inc=1, device_id=device, device_id_type=MESH)

    local = {}

    def local_copy(key, src, dst, sem):
        local[key] = pltpu.make_async_copy(src, dst, sem)
        local[key].start()

    cols = pl.ds(pl.multiple_of(c * 256, 256), 256)
    local_copy("op", oproj, OPW.at[c], S["weights"].at[0])
    local_copy("jw", joinw, JW.at[:, cols], S["weights"].at[1])
    local_copy("hw", headw, HW.at[c], S["weights"].at[2])
    for k in range(C):
        for t, tap in enumerate((low, mid)):
            local_copy(("tap", k, t), tap.at[c, :, k], T.at[t, z, :, k, :, cols], S["tap_own"].at[k, t])
        local_copy(("own", k), attn.at[k], G1.at[k, b, a], S["own"].at[k])
    for h in range(2):
        row = pl.ds(2 * c + h, 1)
        IDS[2 * h:2 * h + 2] = jnp.transpose(jnp.broadcast_to(tgt[row], (128, 128))).reshape(2, C, 16, 128)
    pl.semaphore_wait(barrier, len(partners))

    waited = set()

    def ready(name):
        if name in waited:
            return
        waited.add(name)
        other = pl.ds(pl.multiple_of((1 - c) * 256, 256), 256)
        slots = {"op": OPW.at[1 - c], "jw": JW.at[:, other], "hw": HW.at[1 - c]}
        local[name].wait()
        arrived("sib", (list(slots).index(name),), slots[name])

    def gather_own(n, G, k, own):
        for j in (1, 3, 2):
            send(n + "1", (k, j - 1), own, G.at[k, b, a], along_a(j))
        send(n + "2", (k, 0, 0), own, G.at[k, b, a], along_b(1))
        send(n + "2", (k, 1, 0), own, G.at[k, b, a], along_b(3))

    def gather_line(n, G, k, steps):
        for j in steps:
            slot = G.at[k, b, (a + 4 - j) % 4]
            arrived(n + "1", (k, j - 1), slot)
            send(n + "2", (k, 0, j), slot, slot, along_b(1))
            send(n + "2", (k, 1, j), slot, slot, along_b(3))

    def gather_near(n, G, k, steps):
        for j in steps:
            for d, way in ((0, 1), (1, 3)):
                slot = G.at[k, (b + 4 - way) % 4, (a + 4 - j) % 4]
                arrived(n + "2", (k, d, j), slot)
                if (j in (0, 2)) == (d == 0):
                    send(n + "3", (k, j), slot, slot, along_b(way))

    def gather_far(n, G, k):
        for j in (0, 1, 3, 2):
            arrived(n + "3", (k, j), G.at[k, (b + 2) % 4, (a + 4 - j) % 4])

    def a_own(k):
        gather_own("a", G1, k, attn.at[k])

    def mm1(k):
        local[("own", k)].wait()
        ready("op")
        gather_far("a", G1, k)
        rows = G1[k].reshape(256, 2048)
        for p in range(2):
            part = jnp.dot(rows, OPW[p], preferred_element_type=F32).astype(BF16)
            part = part.reshape(4, 4, 16, 256)
            for i in range(4):
                for h in range(4):
                    P1[k, (1 - c) * h + c * i, (1 - c) * i + c * h, :, p * 256:(p + 1) * 256] = part[i, h]
        for j in (1, 3, 2):
            to = (z + j) % 4
            send("zr", (k, j - 1), P1.at[k, to], RH.at[k, j - 1], along_z(j))

    def high(k):
        for t in range(2):
            local[("tap", k, t)].wait()
            for j, e in z_partners:
                from_cols = pl.ds(pl.multiple_of(((c + e) % 2) * 256, 256), 256)
                arrived("tap", (k, t, e, j), T.at[t, (z + 4 - j) % 4, :, k, :, from_cols])
        for j in (1, 3, 2):
            arrived("zr", (k, j - 1), RH.at[k, j - 1])
        total = P1[k, z].astype(F32)
        for j in range(3):
            total += RH[k, j].astype(F32)
        T[2, z, :, k] = (T[1, z, :, k].astype(F32) + total).astype(BF16)
        for j in (1, 3, 2):
            slot = T.at[2, z, :, k]
            send("zg", (k, j - 1), slot, slot, along_z(j))

    def mm2(k):
        ready("jw")
        for j in (1, 3, 2):
            arrived("zg", (k, j - 1), T.at[2, (z + 4 - j) % 4, :, k])

        @pl.loop(0, 4)
        def _(n):
            wide = pl.ds(pl.multiple_of(n * 512, 512), 512)
            acc = jnp.zeros((256, 512), F32)
            for t in range(3):
                acc += jnp.dot(T[t, :, :, k].reshape(256, 512), JW[t, :, wide], preferred_element_type=F32)
            acc = acc.astype(BF16).reshape(4, 4, 16, 512)
            for i in range(4):
                for h in range(4):
                    P2[k, (1 - c) * h + c * i, (1 - c) * i + c * h, :, wide] = acc[i, h]

        far, up, down = (b + 2) % 4, (b + 1) % 4, (b + 3) % 4
        send("rf", (k, 0), P2.at[k, far, 0:2], RF.at[k, 0], along_b(1))
        send("rf", (k, 1), P2.at[k, far, 2:4], RF.at[k, 1], along_b(3))
        send("rn", (k, 0, 1), P2.at[k, up, 2:4], RN.at[k, 0, 2:4], along_b(1))
        send("rn", (k, 1, 0), P2.at[k, down, 0:2], RN.at[k, 1, 0:2], along_b(3))

    def far(k):
        for d, way, lo in ((0, 1, 0), (1, 3, 2)):
            to = (b + way) % 4
            arrived("rf", (k, d), RF.at[k, d])
            both = P2[k, to, lo:lo + 2].astype(F32) + RF[k, d].astype(F32)
            P2[k, to, lo:lo + 2] = both.astype(BF16)
            send("rn", (k, d, lo // 2), P2.at[k, to, lo:lo + 2], RN.at[k, d, lo:lo + 2], along_b(way))

    def near(k):
        for d in range(2):
            for h in range(2):
                arrived("rn", (k, d, h), RN.at[k, d, 2 * h:2 * h + 2])
        for h in range(4):
            total = P2[k, b, h].astype(F32) + RN[k, 0, h].astype(F32) + RN[k, 1, h].astype(F32)
            Q[k, h] = total.astype(BF16)
        for j in (1, 3, 2):
            send("ra", (k, j - 1), Q.at[k, (a + j) % 4], RA.at[k, j - 1], along_a(j))

    def join(k):
        for j in (1, 3, 2):
            arrived("ra", (k, j - 1), RA.at[k, j - 1])
        total = P2[k, b, a].astype(F32) + RN[k, 0, a].astype(F32) + RN[k, 1, a].astype(F32)
        for j in range(3):
            total += RA[k, j].astype(F32)
        J[k] = total
        SQ[k, 3] = jnp.broadcast_to(jnp.sum(total * total, axis=1, keepdims=True), (16, 128))
        G2[k, b, a] = total.astype(BF16)
        gather_own("h", G2, k, G2.at[k, b, a])
        for j in (1, 3, 2):
            send("sq", (k, j - 1), SQ.at[k, 3], SQ.at[k, j - 1], along_z(j))

    def norm(k):
        for j in (1, 3, 2):
            arrived("sq", (k, j - 1), SQ.at[k, j - 1])
        squares = SQ[k, 0] + SQ[k, 1] + SQ[k, 2] + SQ[k, 3]
        scale = lax.rsqrt(squares[:, 0:1] / WIDTH + 1e-05)
        out[k] = (J[k] * scale * gain[...]).astype(BF16)

    def mm3(k):
        ready("hw")
        gather_far("h", G2, k)
        joined = G2[k].reshape(256, 2048).astype(F32)
        H[...] = (joined * gain[...]).astype(BF16)
        squares = jnp.broadcast_to(jnp.sum(joined * joined, axis=1, keepdims=True), (256, 128))
        squares = squares.reshape(4, 4, 16, 128)
        for i in range(4):
            for h in range(4):
                SS[k, (1 - c) * h + c * i, (1 - c) * i + c * h] = squares[i, h]
        for j in (1, 3, 2):
            send("ss", (k, j - 1), SS.at[k, (z + j) % 4], SZ.at[k, j - 1], along_z(j))
        for p in range(2):
            for lo, hi in ((0, 256), (256, 512), (512, 768), (768, 1000)):
                part = lax.dot_general(
                    H[...], HW[p, lo:hi], (((1,), (1,)), ((), ())), preferred_element_type=F32
                ).astype(BF16)
                part = part.reshape(4, 4, 16, hi - lo)
                for i in range(4):
                    for h in range(4):
                        P3[k, (1 - c) * h + c * i, p, (1 - c) * i + c * h, :, lo:hi] = part[i, h]
            send("lf", (k, p), P3.at[k, (z + 2) % 4, p], LF.at[k, p], along_z(ways[p]))
            send("ln", (k, 1 - p, p), P3.at[k, (z + ways[1 - p]) % 4, p], LN.at[k, 1 - p, p], along_z(ways[1 - p]))

    ways = (1, 3)

    def logits_far(k):
        for p in range(2):
            to = (z + ways[p]) % 4
            arrived("lf", (k, p), LF.at[k, p])
            P3[k, to, p] = (P3[k, to, p].astype(F32) + LF[k, p].astype(F32)).astype(BF16)
            send("ln", (k, p, p), P3.at[k, to, p], LN.at[k, p, p], along_z(ways[p]))

    lane = lax.broadcasted_iota(jnp.int32, (64, 128), 1)

    def packed(top, total, picked):
        return jnp.where(lane == 0, top, jnp.where(lane == 1, total, picked))

    def loss(k):
        for j in (1, 3, 2):
            arrived("ss", (k, j - 1), SZ.at[k, j - 1])
        squares = SS[k, z] + SZ[k, 0] + SZ[k, 1] + SZ[k, 2]
        scale = lax.rsqrt(squares.reshape(64, 128)[:, 0:1] / WIDTH + 1e-05)
        ids = IDS[:, k].reshape(64, 128)[:, 0:1]
        logits, picked = [], jnp.zeros((64, 1), F32)
        for p in range(2):
            total = P3[k, z, p].astype(F32)
            for d in (1 - p, p):
                arrived("ln", (k, d, p), LN.at[k, d, p])
                total += LN[k, d, p].astype(F32)
            total = total.reshape(64, 1000) * scale
            here = lax.broadcasted_iota(jnp.int32, (64, 1000), 1) + ((x * 2 + p) * 4 + g) * 1000
            picked += jnp.sum(jnp.where(here == ids, total, 0.0), axis=1, keepdims=True)
            logits.append(total)
        top = jnp.maximum(*(jnp.max(v, axis=1, keepdims=True) for v in logits))
        total = sum(jnp.sum(jnp.exp(v - top), axis=1, keepdims=True) for v in logits)
        STATS[:, k] = packed(top, total, picked).reshape(4, 16, 128)

    def finish():
        for h in range(2):
            ST[0, 0, h] = jnp.transpose(STATS[2 * h:2 * h + 2].reshape(128, 128))[0:8]
        for i, j in plane:
            send("st", (i, j), ST.at[0, 0], ST.at[i, j], in_plane(i, j))
        for i, j in plane:
            arrived("st", (i, j), ST.at[i, j])
        for e in range(2):
            of = (c + e) % 2
            for h in range(2):
                parts = [ST[i, j, h] for i in range(e, 8, 2) for j in range(4)]
                top = functools.reduce(jnp.maximum, [v[0:1] for v in parts])
                total = sum(v[1:2] * jnp.exp(v[0:1] - top) for v in parts)
                picked = sum(v[2:3] for v in parts)
                row = pl.ds(2 * of + h, 1)
                loss_out[row] = msk[row].astype(F32) * (top + jnp.log(total) - picked)

    z_partners = [(0, 1), (2, 0), (2, 1), (1, 0), (1, 1), (3, 0), (3, 1)]

    def taps_far(k):
        taps(k, [(2, 0), (2, 1)])

    def taps(k, partners=((0, 1), (1, 0), (1, 1), (3, 0), (3, 1))):
        for j, e in partners:
            for t, tap in enumerate((low, mid)):
                slot = T.at[t, z, :, k, :, cols]
                send("tap", (k, t, e, j), tap.at[(c + e) % 2, :, k], slot, along_z(j, e))
        if k == 0 and (0, 1) in partners:
            send("sib", (0,), oproj, OPW.at[c], sib)
            send("sib", (1,), joinw, JW.at[:, cols], sib)
            send("sib", (2,), headw, HW.at[c], sib)

    fns = dict(
        taps=taps, taps_far=taps_far, lfar=logits_far, a_own=a_own, mm1=mm1, high=high, mm2=mm2, far=far, near=near, join=join, norm=norm, mm3=mm3, loss=loss,
    )
    for n, G in (("a", G1), ("h", G2)):
        fns[n + "_line"] = functools.partial(gather_line, n, G, steps=(1, 3))
        fns[n + "_far_line"] = functools.partial(gather_line, n, G, steps=(2,))
        fns[n + "_near0"] = functools.partial(gather_near, n, G, steps=(0,))
        fns[n + "_near"] = functools.partial(gather_near, n, G, steps=(1, 3))
        fns[n + "_near2"] = functools.partial(gather_near, n, G, steps=(2,))
    for n, k in ORDER:
        fns[n](k)
    finish()
    for copy in sent:
        copy.wait_send()


def on_device(attn_heads, out_proj, low_tap, mid_tap, join_weight, norm_gain, head_weight, targets, loss_mask):
    anywhere = pl.BlockSpec(memory_space=pl.ANY)
    vmem = pl.BlockSpec(memory_space=pltpu.VMEM)
    sems = [pltpu.SemaphoreType.DMA(s) for s in SEMS.values()]
    sems += [pltpu.SemaphoreType.DMA(s) for s in PAIRS.values() for _ in range(2)]
    hidden, loss = pl.pallas_call(
        kernel,
        name="draft_head",
        out_shape=(
            jax.ShapeDtypeStruct((C, 16, 2048), BF16),
            jax.ShapeDtypeStruct((4, 128), F32),
        ),
        in_specs=[anywhere] * 6 + [vmem] * 3,
        out_specs=(vmem, vmem),
        scratch_shapes=[pltpu.VMEM(*s) for s in BUFS.values()] + sems,
        compiler_params=pltpu.CompilerParams(collective_id=0, has_side_effects=True, vmem_limit_bytes=60 << 20),
    )(
        attn_heads.reshape(C, 16, 2048),
        out_proj,
        low_tap.reshape(2, 4, C, 16, 256),
        mid_tap.reshape(2, 4, C, 16, 256),
        join_weight,
        head_weight.T,
        norm_gain.reshape(1, 2048),
        targets.reshape(4, 128),
        loss_mask.reshape(4, 128),
    )
    return hidden.reshape(64, 2048), loss.reshape(512)


def solution(mesh):
    in_specs = (
        P(("dp", "group"), "tensor"),
        P("tensor", ("dp", "group")),
        P("tensor", ("dp", "group")),
        P("tensor", ("dp", "group")),
        P(None, ("dp", "group"), "tensor"),
        P("tensor"),
        P("tensor", ("dp", "group")),
        P("tensor"),
        P("tensor"),
    )
    out_specs = (P(("dp", "group"), "tensor"), P("tensor"))
    return jax.shard_map(
        on_device, mesh=mesh, in_specs=in_specs, out_specs=out_specs, check_vma=False
    )
```

```python
import functools

import jax
import jax.numpy as jnp
from jax import lax
from jax.experimental import pallas as pl
from jax.experimental.pallas import tpu as pltpu
from jax.sharding import PartitionSpec as P

MESH = pl.DeviceIdType.MESH
C = 4
F32 = jnp.float32
BF16 = jnp.bfloat16
WIDTH = 8192
BEHIND = 14

ORDER = (
    ("a_own", 3), ("taps", 1), ("a_own", 1), ("taps", 3), ("a_line", 3), ("a_far_line", 3), ("taps", 0),
    ("a_near0", 3), ("a_line", 1), ("a_far_line", 1), ("a_near", 3), ("taps_far", 3), ("taps_far", 1),
    ("a_near2", 3), ("a_own", 0), ("taps_far", 0), ("a_near0", 1), ("a_near", 1), ("a_near2", 1), ("mm1", 3),
    ("a_line", 0), ("a_far_line", 0), ("a_own", 2), ("mm1", 1), ("a_near0", 0), ("a_near", 0), ("a_near2", 0),
    ("a_line", 2), ("high", 3), ("a_far_line", 2), ("mm1", 0), ("a_near0", 2), ("a_near", 2), ("high", 1),
    ("mm2", 3), ("a_near2", 2), ("high", 0), ("taps", 2), ("far", 3), ("mm2", 1), ("mm1", 2), ("near", 3),
    ("mm2", 0), ("far", 1), ("join", 3), ("high", 2), ("far", 0), ("near", 1), ("h_line", 3), ("taps_far", 2),
    ("h_far_line", 3), ("near", 0), ("join", 1), ("h_near0", 3), ("h_near", 3), ("h_near2", 3), ("mm2", 2),
    ("h_line", 1), ("h_far_line", 1), ("join", 0), ("mm3", 3), ("far", 2), ("h_near0", 1), ("h_near", 1),
    ("h_near2", 1), ("h_line", 0), ("h_far_line", 0), ("norm", 3), ("near", 2), ("lfar", 3), ("lfar1", 3),
    ("h_near0", 0), ("mm3", 1), ("h_near", 0), ("h_near2", 0), ("join", 2), ("mm3", 0), ("h_line", 2),
    ("h_far_line", 2), ("norm", 2), ("lfar", 1), ("lfar1", 1), ("h_near0", 2), ("lfar", 0), ("norm", 0),
    ("h_near", 2), ("h_near2", 2), ("lfar1", 0), ("mm3", 2), ("loss", 3), ("loss", 0), ("loss", 1),
    ("lfar", 2), ("lfar1", 2), ("norm", 1), ("loss", 2),
)

SEMS = {
    "own": (C,),
    "weights": (3,),
    "tap_own": (C, 2),
}
PAIRS = {
    "sib": (3,),
    "tap": (C, 2, 2, 4),
    "tf": (C, 2),
    "a1": (C, 3),
    "a2": (C, 2, 4),
    "a3": (C, 4),
    "h1": (C, 3),
    "h2": (C, 2, 4),
    "h3": (C, 4),
    "zr": (C, 3),
    "zg": (C, 3),
    "rf": (C, 2),
    "rn": (C, 2, 2),
    "ra": (C, 3),
    "sq": (C, 3),
    "lf": (C, 2),
    "ln": (C, 2, 2),
    "ss": (C, 3),
    "st": (8, 4),
}
BUFS = {
    "G1": ((C, 4, 4, 16, 2048), BF16),
    "G2": ((C, 4, 4, 16, 2048), BF16),
    "OPW": ((2, 2048, 256), BF16),
    "JW": ((3, 512, 2048), BF16),
    "HW": ((2, 1000, 2048), BF16),
    "T": ((3, 4, 4, C, 16, 512), BF16),
    "P1": ((C, 4, 4, 16, 512), BF16),
    "RH": ((C, 3, 4, 16, 512), BF16),
    "P2": ((C, 4, 4, 16, 2048), BF16),
    "RF": ((C, 2, 2, 16, 2048), BF16),
    "RN": ((C, 2, 4, 16, 2048), BF16),
    "Q": ((C, 4, 16, 2048), BF16),
    "RA": ((C, 3, 16, 2048), BF16),
    "J": ((C, 16, 2048), F32),
    "SQ": ((C, 4, 16, 128), F32),
    "H": ((256, 2048), BF16),
    "SS": ((C, 4, 8, 128), F32),
    "SC": ((4, 4, 16, 128), F32),
    "P3": ((C, 4, 2, 4, 16, 1000), BF16),
    "LF": ((C, 2, 4, 16, 1000), BF16),
    "LN": ((C, 2, 2, 4, 16, 1000), BF16),
    "STATS": ((4, C, 16, 128), F32),
    "ST": ((8, 4, 2, 8, 128), F32),
    "IDS": ((4, C, 16, 128), jnp.int32),
}


def kernel(attn, oproj, low, mid, joinw, headw, gain, tgt, msk, out, loss_out, *scratch):
    names = list(BUFS) + list(SEMS) + [n + s for n in PAIRS for s in ("_s", "_r")]
    S = dict(zip(names, scratch))
    G1, G2, OPW, JW, HW, T = (S[n] for n in ("G1", "G2", "OPW", "JW", "HW", "T"))
    P1, RH, P2, RF, RN, Q, RA, J = (S[n] for n in ("P1", "RH", "P2", "RF", "RN", "Q", "RA", "J"))
    SQ, P3, LF, LN, H, SS, SC = (S[n] for n in ("SQ", "P3", "LF", "LN", "H", "SS", "SC"))
    IDS, STATS, ST = (S[n] for n in ("IDS", "STATS", "ST"))

    dp, z, g = lax.axis_index("dp"), lax.axis_index("tensor"), lax.axis_index("group")
    x, c = dp // 2, dp % 2
    a = (1 - c) * x + c * g
    b = (1 - c) * g + c * x

    def place(x, c, z, g):
        return (x * 2 + c, z, g)

    def along_a(j):
        return place((x + (1 - c) * j) % 4, c, z, (g + c * j) % 4)

    def along_b(j):
        return place((x + c * j) % 4, c, z, (g + (1 - c) * j) % 4)

    def along_z(j, e=0):
        return place(x, (c + e) % 2, (z + j) % 4, g)

    sib = along_z(0, 1)
    sent, marks, flushed = [], [], [0]

    def flush(upto):
        for copy in sent[flushed[0]:upto]:
            copy.wait_send()
        flushed[0] = max(flushed[0], upto)

    def send(name, index, src, dst, device):
        copy = pltpu.make_async_remote_copy(
            src_ref=src, dst_ref=dst, send_sem=S[name + "_s"].at[index],
            recv_sem=S[name + "_r"].at[index], device_id=device, device_id_type=MESH,
        )
        copy.start()
        sent.append(copy)

    def arrived(name, index, slot):
        pltpu.make_async_remote_copy(
            src_ref=slot, dst_ref=slot, send_sem=S[name + "_s"].at[index],
            recv_sem=S[name + "_r"].at[index], device_id=sib, device_id_type=MESH,
        ).wait_recv()

    barrier = pltpu.get_barrier_semaphore()
    plane = [(i, j) for i in range(8) for j in range(4) if (i, j) != (0, 0)]

    def in_plane(i, j):
        return ((dp + i) % 8, z, (g + j) % 4)

    partners = [in_plane(i, j) for i, j in plane]
    partners += [along_z(j, e) for e in (0, 1) for j in (1, 2, 3)]
    for device in partners:
        pl.semaphore_signal(barrier, inc=1, device_id=device, device_id_type=MESH)

    local = {}

    def local_copy(key, src, dst, sem):
        local[key] = pltpu.make_async_copy(src, dst, sem)
        local[key].start()

    cols = pl.ds(pl.multiple_of(c * 256, 256), 256)
    local_copy("op", oproj, OPW.at[c], S["weights"].at[0])
    local_copy("jw", joinw, JW.at[:, cols], S["weights"].at[1])
    local_copy("hw", headw, HW.at[c], S["weights"].at[2])
    for k in range(C):
        for t, tap in enumerate((low, mid)):
            local_copy(("tap", k, t), tap.at[c, :, k], T.at[t, z, :, k, :, cols], S["tap_own"].at[k, t])
        local_copy(("own", k), attn.at[k], G1.at[k, b, a], S["own"].at[k])
    for h in range(2):
        row = pl.ds(2 * c + h, 1)
        IDS[2 * h:2 * h + 2] = jnp.transpose(jnp.broadcast_to(tgt[row], (128, 128))).reshape(2, C, 16, 128)
    pl.semaphore_wait(barrier, len(partners))

    waited = set()

    def ready(name):
        if name in waited:
            return
        waited.add(name)
        other = pl.ds(pl.multiple_of((1 - c) * 256, 256), 256)
        slots = {"op": OPW.at[1 - c], "jw": JW.at[:, other], "hw": HW.at[1 - c]}
        local[name].wait()
        arrived("sib", (list(slots).index(name),), slots[name])

    def gather_own(n, G, k, own):
        for j in (1, 3, 2):
            send(n + "1", (k, j - 1), own, G.at[k, b, a], along_a(j))
        send(n + "2", (k, 0, 0), own, G.at[k, b, a], along_b(1))
        send(n + "2", (k, 1, 0), own, G.at[k, b, a], along_b(3))

    def gather_line(n, G, k, steps):
        for j in steps:
            slot = G.at[k, b, (a + 4 - j) % 4]
            arrived(n + "1", (k, j - 1), slot)
            send(n + "2", (k, 0, j), slot, slot, along_b(1))
            send(n + "2", (k, 1, j), slot, slot, along_b(3))

    def gather_near(n, G, k, steps):
        for j in steps:
            for d, way in ((0, 1), (1, 3)):
                slot = G.at[k, (b + 4 - way) % 4, (a + 4 - j) % 4]
                arrived(n + "2", (k, d, j), slot)
                if (j in (0, 2)) == (d == 0):
                    send(n + "3", (k, j), slot, slot, along_b(way))

    def gather_far(n, G, k):
        for j in (0, 1, 3, 2):
            arrived(n + "3", (k, j), G.at[k, (b + 2) % 4, (a + 4 - j) % 4])

    def a_own(k):
        gather_own("a", G1, k, attn.at[k])

    def mm1(k):
        local[("own", k)].wait()
        ready("op")
        gather_far("a", G1, k)
        rows = G1[k].reshape(256, 2048)
        for p in range(2):
            part = jnp.dot(rows, OPW[p], preferred_element_type=F32).astype(BF16)
            part = part.reshape(4, 4, 16, 256)
            for i in range(4):
                for h in range(4):
                    P1[k, (1 - c) * h + c * i, (1 - c) * i + c * h, :, p * 256:(p + 1) * 256] = part[i, h]
        for j in (1, 3, 2):
            to = (z + j) % 4
            send("zr", (k, j - 1), P1.at[k, to], RH.at[k, j - 1], along_z(j))

    def high(k):
        local[("tap", k, 1)].wait()
        arrived("tap", (k, 1, 1, 0), tap_slot(1, 0, k, 1))
        for j in (1, 3, 2):
            arrived("zr", (k, j - 1), RH.at[k, j - 1])
        total = P1[k, z].astype(F32)
        for j in range(3):
            total += RH[k, j].astype(F32)
        T[2, z, :, k] = (T[1, z, :, k].astype(F32) + total).astype(BF16)
        for j in (1, 3, 2):
            slot = T.at[2, z, :, k]
            send("zg", (k, j - 1), slot, slot, along_z(j))

    def mm2(k):
        ready("jw")
        local[("tap", k, 0)].wait()
        arrived("tap", (k, 0, 1, 0), tap_slot(0, 0, k, 1))
        for t, j in ((0, 3), (1, 1)):
            for e in range(2):
                arrived("tap", (k, t, e, j), tap_slot(t, j, k, e))
        for t in range(2):
            arrived("tf", (k, t), T.at[t, (z + 2) % 4, :, k])
        for j in (1, 3, 2):
            arrived("zg", (k, j - 1), T.at[2, (z + 4 - j) % 4, :, k])

        @pl.loop(0, 4)
        def _(n):
            wide = pl.ds(pl.multiple_of(n * 512, 512), 512)
            acc = jnp.zeros((256, 512), F32)
            for t in range(3):
                acc += jnp.dot(T[t, :, :, k].reshape(256, 512), JW[t, :, wide], preferred_element_type=F32)
            acc = acc.astype(BF16).reshape(4, 4, 16, 512)
            for i in range(4):
                for h in range(4):
                    P2[k, (1 - c) * h + c * i, (1 - c) * i + c * h, :, wide] = acc[i, h]

        far, up, down = (b + 2) % 4, (b + 1) % 4, (b + 3) % 4
        send("rf", (k, 0), P2.at[k, far, 0:2], RF.at[k, 0], along_b(1))
        send("rf", (k, 1), P2.at[k, far, 2:4], RF.at[k, 1], along_b(3))
        send("rn", (k, 0, 1), P2.at[k, up, 2:4], RN.at[k, 0, 2:4], along_b(1))
        send("rn", (k, 1, 0), P2.at[k, down, 0:2], RN.at[k, 1, 0:2], along_b(3))

    def far(k):
        for d, way, lo in ((0, 1, 0), (1, 3, 2)):
            to = (b + way) % 4
            arrived("rf", (k, d), RF.at[k, d])
            both = P2[k, to, lo:lo + 2].astype(F32) + RF[k, d].astype(F32)
            P2[k, to, lo:lo + 2] = both.astype(BF16)
            send("rn", (k, d, lo // 2), P2.at[k, to, lo:lo + 2], RN.at[k, d, lo:lo + 2], along_b(way))

    def near(k):
        for d in range(2):
            for h in range(2):
                arrived("rn", (k, d, h), RN.at[k, d, 2 * h:2 * h + 2])
        for h in range(4):
            total = P2[k, b, h].astype(F32) + RN[k, 0, h].astype(F32) + RN[k, 1, h].astype(F32)
            Q[k, h] = total.astype(BF16)
        for j in (1, 3, 2):
            send("ra", (k, j - 1), Q.at[k, (a + j) % 4], RA.at[k, j - 1], along_a(j))

    def join(k):
        for j in (1, 3, 2):
            arrived("ra", (k, j - 1), RA.at[k, j - 1])
        total = P2[k, b, a].astype(F32) + RN[k, 0, a].astype(F32) + RN[k, 1, a].astype(F32)
        for j in range(3):
            total += RA[k, j].astype(F32)
        J[k] = total
        SQ[k, 3] = jnp.broadcast_to(jnp.sum(total * total, axis=1, keepdims=True), (16, 128))
        G2[k, b, a] = total.astype(BF16)
        gather_own("h", G2, k, G2.at[k, b, a])
        for j in (1, 3, 2):
            send("sq", (k, j - 1), SQ.at[k, 3], SQ.at[k, j - 1], along_z(j))

    def norm(k):
        for j in (1, 3, 2):
            arrived("sq", (k, j - 1), SQ.at[k, j - 1])
        squares = SQ[k, 0] + SQ[k, 1] + SQ[k, 2] + SQ[k, 3]
        scale = lax.rsqrt(squares[:, 0:1] / WIDTH + 1e-05)
        out[k] = (J[k] * scale * gain[...]).astype(BF16)

    def mm3(k):
        ready("hw")
        gather_far("h", G2, k)
        joined = G2[k].reshape(256, 2048).astype(F32)
        H[...] = (joined * gain[...]).astype(BF16)
        squares = jnp.broadcast_to(jnp.sum(joined * joined, axis=1, keepdims=True), (256, 128))
        for h in range(2):
            across = jnp.transpose(squares[128 * h:128 * h + 128])
            SS[k, 3, 4 * h:4 * h + 4] = across[0:4]
        for p in range(2):
            for lo, hi in ((0, 256), (256, 512), (512, 768), (768, 1000)):
                part = lax.dot_general(
                    H[...], HW[p, lo:hi], (((1,), (1,)), ((), ())), preferred_element_type=F32
                ).astype(BF16)
                part = part.reshape(4, 4, 16, hi - lo)
                for i in range(4):
                    for h in range(4):
                        P3[k, (1 - c) * h + c * i, p, (1 - c) * i + c * h, :, lo:hi] = part[i, h]
            send("lf", (k, p), P3.at[k, (z + 2) % 4, p], LF.at[k, p], along_z(ways[p]))
        for p in range(2):
            send("ln", (k, 1 - p, p), P3.at[k, (z + ways[1 - p]) % 4, p], LN.at[k, 1 - p, p], along_z(ways[1 - p]))
        for j in (1, 3, 2):
            send("ss", (k, j - 1), SS.at[k, 3], SS.at[k, j - 1], along_z(j))

    ways = (1, 3)

    def logits_far(k, p):
        to = (z + ways[p]) % 4
        arrived("lf", (k, p), LF.at[k, p])
        P3[k, to, p] = (P3[k, to, p].astype(F32) + LF[k, p].astype(F32)).astype(BF16)
        send("ln", (k, p, p), P3.at[k, to, p], LN.at[k, p, p], along_z(ways[p]))

    lane = lax.broadcasted_iota(jnp.int32, (64, 128), 1)

    def packed(top, total, picked):
        return jnp.where(lane == 0, top, jnp.where(lane == 1, total, picked))

    def loss(k):
        for j in (1, 3, 2):
            arrived("ss", (k, j - 1), SS.at[k, j - 1])
        squares = SS[k, 0] + SS[k, 1] + SS[k, 2] + SS[k, 3]
        for h in range(2):
            down = jnp.transpose(jnp.broadcast_to(squares[4 * h:4 * h + 1], (128, 128)))
            SC[2 * h:2 * h + 2] = down.reshape(2, 4, 16, 128)
        squares = jnp.concatenate([SC[(1 - c) * i + c * z, (1 - c) * z + c * i] for i in range(4)], axis=0)
        scale = lax.rsqrt(squares[:, 0:1] / WIDTH + 1e-05)
        ids = IDS[:, k].reshape(64, 128)[:, 0:1]
        logits, picked = [], jnp.zeros((64, 1), F32)
        for p in range(2):
            total = P3[k, z, p].astype(F32)
            for d in (1 - p, p):
                arrived("ln", (k, d, p), LN.at[k, d, p])
                total += LN[k, d, p].astype(F32)
            total = total.reshape(64, 1000) * scale
            here = lax.broadcasted_iota(jnp.int32, (64, 1000), 1) + ((x * 2 + p) * 4 + g) * 1000
            picked += jnp.sum(jnp.where(here == ids, total, 0.0), axis=1, keepdims=True)
            logits.append(total)
        top = jnp.maximum(*(jnp.max(v, axis=1, keepdims=True) for v in logits))
        total = sum(jnp.sum(jnp.exp(v - top), axis=1, keepdims=True) for v in logits)
        STATS[:, k] = packed(top, total, picked).reshape(4, 16, 128)

    def finish():
        for h in range(2):
            ST[0, 0, h] = jnp.transpose(STATS[2 * h:2 * h + 2].reshape(128, 128))[0:8]
        for i, j in plane:
            send("st", (i, j), ST.at[0, 0], ST.at[i, j], in_plane(i, j))
        flush(len(sent) - len(plane))
        for i, j in plane:
            arrived("st", (i, j), ST.at[i, j])
        for e in range(2):
            of = (c + e) % 2
            for h in range(2):
                parts = [ST[i, j, h] for i in range(e, 8, 2) for j in range(4)]
                top = functools.reduce(jnp.maximum, [v[0:1] for v in parts])
                total = sum(v[1:2] * jnp.exp(v[0:1] - top) for v in parts)
                picked = sum(v[2:3] for v in parts)
                row = pl.ds(2 * of + h, 1)
                loss_out[row] = msk[row].astype(F32) * (top + jnp.log(total) - picked)

    z_partners = [(0, 1), (1, 0), (3, 0), (1, 1), (3, 1)]

    def tap_slot(t, j, k, e):
        from_cols = pl.ds(pl.multiple_of(((c + e) % 2) * 256, 256), 256)
        return T.at[t, (z + 4 - j) % 4, :, k, :, from_cols]

    def taps_far(k):
        for t, j in ((0, 1), (1, 3)):
            for e in range(2):
                arrived("tap", (k, t, e, j), tap_slot(t, j, k, e))
            slot = T.at[t, (z + 4 - j) % 4, :, k]
            send("tf", (k, t), slot, slot, along_z(j))

    def taps(k):
        for j, e in z_partners:
            for t, tap in enumerate((low, mid)):
                slot = T.at[t, z, :, k, :, cols]
                send("tap", (k, t, e, j), tap.at[(c + e) % 2, :, k], slot, along_z(j, e))
        if k == 0:
            send("sib", (0,), oproj, OPW.at[c], sib)
            send("sib", (1,), joinw, JW.at[:, cols], sib)
            send("sib", (2,), headw, HW.at[c], sib)

    fns = dict(
        taps=taps, taps_far=taps_far, a_own=a_own, mm1=mm1, high=high, mm2=mm2, far=far, near=near, join=join,
        norm=norm, mm3=mm3, loss=loss,
        lfar=functools.partial(logits_far, p=0), lfar1=functools.partial(logits_far, p=1),
    )
    for n, G in (("a", G1), ("h", G2)):
        fns[n + "_line"] = functools.partial(gather_line, n, G, steps=(1, 3))
        fns[n + "_far_line"] = functools.partial(gather_line, n, G, steps=(2,))
        fns[n + "_near0"] = functools.partial(gather_near, n, G, steps=(0,))
        fns[n + "_near"] = functools.partial(gather_near, n, G, steps=(1, 3))
        fns[n + "_near2"] = functools.partial(gather_near, n, G, steps=(2,))
    for n, k in ORDER:
        fns[n](k)
        marks.append(len(sent))
        if len(marks) > BEHIND:
            flush(marks[-1 - BEHIND])
    finish()
    flush(len(sent))


def on_device(attn_heads, out_proj, low_tap, mid_tap, join_weight, norm_gain, head_weight, targets, loss_mask):
    anywhere = pl.BlockSpec(memory_space=pl.ANY)
    vmem = pl.BlockSpec(memory_space=pltpu.VMEM)
    sems = [pltpu.SemaphoreType.DMA(s) for s in SEMS.values()]
    sems += [pltpu.SemaphoreType.DMA(s) for s in PAIRS.values() for _ in range(2)]
    hidden, loss = pl.pallas_call(
        kernel,
        name="draft_head",
        out_shape=(
            jax.ShapeDtypeStruct((C, 16, 2048), BF16),
            jax.ShapeDtypeStruct((4, 128), F32),
        ),
        in_specs=[anywhere] * 6 + [vmem] * 3,
        out_specs=(vmem, vmem),
        scratch_shapes=[pltpu.VMEM(*s) for s in BUFS.values()] + sems,
        compiler_params=pltpu.CompilerParams(collective_id=0, has_side_effects=True, vmem_limit_bytes=60 << 20),
    )(
        attn_heads.reshape(C, 16, 2048),
        out_proj,
        low_tap.reshape(2, 4, C, 16, 256),
        mid_tap.reshape(2, 4, C, 16, 256),
        join_weight,
        head_weight.T,
        norm_gain.reshape(1, 2048),
        targets.reshape(4, 128),
        loss_mask.reshape(4, 128),
    )
    return hidden.reshape(64, 2048), loss.reshape(512)


def solution(mesh):
    in_specs = (
        P(("dp", "group"), "tensor"),
        P("tensor", ("dp", "group")),
        P("tensor", ("dp", "group")),
        P("tensor", ("dp", "group")),
        P(None, ("dp", "group"), "tensor"),
        P("tensor"),
        P("tensor", ("dp", "group")),
        P("tensor"),
        P("tensor"),
    )
    out_specs = (P(("dp", "group"), "tensor"), P("tensor"))
    return jax.shard_map(
        on_device, mesh=mesh, in_specs=in_specs, out_specs=out_specs, check_vma=False
    )
```
